32 devices in a mesh: seq: 8 (over z, x), head: 4 (over y, core).
Axes of the slice: x: 2, y: 2, z: 4, core: 2. Of those that a mesh axis runs over, the one named last changes fastest.
Arguments:
- query_rows: bfloat16 [16384, 1024], P('seq', 'head'), may hold values from -6 to 6
- key_rows: bfloat16 [16384, 1024], P('seq', 'head'), may hold values from -6 to 6
- value_rows: bfloat16 [16384, 1024], P('seq', 'head'), may hold values from -24 to 24
- norm_gain: bfloat16 [1024], P('head'), may hold values from 0.5 to 1.5
Outputs:
- attended: bfloat16 [16384, 1024], P('seq', 'head')
The draws below stay inside these ranges and needn't reach their ends.
All inputs are finite; a program needn't handle non-finite values.
Results may differ from the reference program's by a relative error of at most 0.01.
Values may be sent and summed in bfloat16 or wider, within the bound.
A program may use at most 192 MiB of HBM per device.

```python
import math
import jax
import jax.numpy as jnp
from jax import lax

D = 1024
HEADS = 16
BLOCK = 1024
LEVELS = 3
TOP_POOL = 32
TOKENS = 16384
N_SEQ = 8


def spread_windows(window_rows):
    return jnp.repeat(window_rows, TOP_POOL, axis=0)


def draw_query_rows(key, part):
    key = jax.random.fold_in(key, 11)
    drawn = jnp.clip(jax.random.normal(key, (TOKENS, D), jnp.float32), -5.0, 5.0)
    return drawn.astype(jnp.bfloat16)


def draw_key_rows(key, part):
    key = jax.random.fold_in(key, 17)
    window_count = TOKENS // TOP_POOL
    window_part = spread_windows(jax.random.normal(jax.random.fold_in(key, 4), (window_count, D), jnp.float32))
    noise_part = jax.random.normal(key, (TOKENS, D), jnp.float32)
    drawn = jnp.clip(1.5 * window_part + 0.7 * noise_part, -6.0, 6.0)
    return drawn.astype(jnp.bfloat16)


def draw_value_rows(key, part):
    key = jax.random.fold_in(key, 23)
    columns = jnp.arange(D, dtype=jnp.float32) / (D - 1)
    spread = jax.random.uniform(jax.random.fold_in(key, 1), (D,), jnp.float32, 0.6, 1.7)
    window_count = TOKENS // TOP_POOL
    rising = jnp.exp(math.log(3.0) * columns)
    noise_part = jnp.clip(jax.random.normal(jax.random.fold_in(key, 2), (TOKENS, D), jnp.float32), -4.0, 4.0)
    window_part = spread_windows(jnp.clip(jax.random.normal(jax.random.fold_in(key, 4), (window_count, D), jnp.float32), -4.0, 4.0))
    drawn = 0.8 * noise_part + 0.9 * window_part
    return jnp.clip(drawn * rising * spread, -24.0, 24.0).astype(jnp.bfloat16)


def setup_inputs(seed: int = 0) -> dict:
    key_list = jax.random.split(jax.random.key(seed), 5)
    return {
        "query_rows": draw_query_rows(jax.random.fold_in(key_list[4], 71), 0),
        "key_rows": draw_key_rows(jax.random.fold_in(key_list[4], 71), 0),
        "value_rows": draw_value_rows(jax.random.fold_in(key_list[4], 71), 0),
        "norm_gain": jnp.clip(1.0 + 0.1 * jax.random.normal(key_list[3], (D,), jnp.float32), 0.5, 1.5).astype(jnp.bfloat16),
    }


def pooled(source, factor):
    row_count = source.shape[0] // factor
    grouped = source.astype(jnp.float32).reshape(row_count, factor, source.shape[1])
    return lax.optimization_barrier(jnp.mean(grouped, axis=1)).astype(jnp.bfloat16)

def attend_part(query_block, key_block, value_block):
    scaling = 1.0 / math.sqrt(query_block.shape[-1])
    scores = jnp.einsum('...qhe,...khe->...hqk', query_block.astype(jnp.float32), key_block.astype(jnp.float32)) * scaling
    highest = lax.optimization_barrier(jnp.max(scores, axis=-1))
    exponent = jnp.exp(scores - highest[..., None])
    denominator = lax.optimization_barrier(jnp.sum(exponent, axis=-1))
    weights = lax.optimization_barrier(exponent.astype(jnp.bfloat16)).astype(jnp.float32)
    summed = jnp.einsum('...hqk,...khe->...hqe', weights, value_block.astype(jnp.float32))
    return (highest, denominator, summed)

def combine(earlier, latter):
    high_first, denom_first, sum_first = earlier
    high_second, denom_second, sum_second = latter
    highest = jnp.maximum(high_first, high_second)
    factor_first = jnp.exp(high_first - highest)
    factor_second = jnp.exp(high_second - highest)
    denominator = denom_first * factor_first + denom_second * factor_second
    summed = sum_first * factor_first[..., None] + sum_second * factor_second[..., None]
    return (highest, denominator, summed)

def reference(query_rows, key_rows, value_rows, norm_gain):
    tokens_all, full_width = query_rows.shape
    tok_count = tokens_all // N_SEQ
    head_count = HEADS
    head_width = full_width // head_count
    coarse_count = tok_count // TOP_POOL
    coarse_keys = pooled(key_rows, TOP_POOL).reshape(N_SEQ, coarse_count, head_count, head_width)
    coarse_values = pooled(value_rows, TOP_POOL).reshape(N_SEQ, coarse_count, head_count, head_width)
    block_count = tok_count // BLOCK

    def one_device(device_number):
        first_row = device_number * tok_count
        query_dev = lax.dynamic_slice_in_dim(query_rows, first_row, tok_count, 0).reshape(tok_count, head_count, head_width)
        key_dev = lax.dynamic_slice_in_dim(key_rows, first_row, tok_count, 0).reshape(tok_count, head_count, head_width)
        value_dev = lax.dynamic_slice_in_dim(value_rows, first_row, tok_count, 0).reshape(tok_count, head_count, head_width)
        block_shape = (block_count, BLOCK, head_count, head_width)
        diag = attend_part(query_dev.reshape(block_shape), key_dev.reshape(block_shape), value_dev.reshape(block_shape))
        partial_value = (jnp.transpose(diag[0], (1, 0, 2)).reshape(head_count, tok_count), jnp.transpose(diag[1], (1, 0, 2)).reshape(head_count, tok_count), jnp.transpose(diag[2], (1, 0, 2, 3)).reshape(head_count, tok_count, head_width))
        for height in range(1, LEVELS + 1):
            partner = jnp.bitwise_xor(device_number, 2 ** (height - 1)).astype(jnp.int32)
            partner_first = (partner * tok_count).astype(jnp.int32)
            other_keys = lax.dynamic_slice_in_dim(key_rows, partner_first, tok_count, 0)
            other_values = lax.dynamic_slice_in_dim(value_rows, partner_first, tok_count, 0)
            pooled_keys = pooled(other_keys, 2 ** height).reshape(-1, head_count, head_width)
            pooled_values = pooled(other_values, 2 ** height).reshape(-1, head_count, head_width)
            partial_value = combine(partial_value, attend_part(query_dev, pooled_keys, pooled_values))

        def fold_source(carried, pieces):
            return (combine(carried, attend_part(query_dev, pieces[0], pieces[1])), None)
        partial_value, _ = lax.scan(fold_source, partial_value, (coarse_keys, coarse_values))
        context = partial_value[2] / partial_value[1][..., None]
        return jnp.transpose(context, (1, 0, 2)).reshape(tok_count, full_width)
    contexts = lax.map(one_device, jnp.arange(N_SEQ, dtype=jnp.int32))
    context = contexts.reshape(tokens_all, full_width)
    mean_square = lax.optimization_barrier(jnp.mean(context * context, axis=-1, keepdims=True))
    attended = context * lax.rsqrt(mean_square + 1e-06) * norm_gain.astype(jnp.float32)
    return attended.astype(jnp.bfloat16)
```

```python
import functools
import math

import jax
import jax.numpy as jnp
from jax import lax
from jax.experimental import pallas as pl
from jax.experimental.pallas import tpu as pltpu
from jax.sharding import PartitionSpec as P

D = 1024
HEAD_DIM = 64
BLOCK = 1024
LEVELS = 3
TOP_POOL = 32
QUERY_TILE = 256
CHUNK = 256
LANES = 128
LOG2E = math.log2(math.e)
MESH = pl.DeviceIdType.MESH


def pool_matrix(factors):
    pieces = []
    for factor in factors:
        shape = (CHUNK // factor, CHUNK)
        row = lax.broadcasted_iota(jnp.int32, shape, 0)
        window = lax.broadcasted_iota(jnp.int32, shape, 1) // factor
        pieces.append(jnp.where(window == row, 1.0 / factor, 0.0))
    return jnp.concatenate(pieces, axis=0).astype(jnp.bfloat16)


def kernel(n_seq, n_head, q_ref, k_ref, v_ref, g_ref, o_ref,
           near, far, acc, high, ctx, squares,
           level_send, level_recv, coarse_send, coarse_recv, square_send, square_recv):
    tokens, width = q_ref.shape
    heads = width // HEAD_DIM
    coarse_rows = tokens // TOP_POOL
    coarse_all = coarse_rows * n_seq
    me_seq = lax.axis_index("seq")
    me_head = lax.axis_index("head")

    def seq_peer(step):
        return lax.rem(me_seq + step, n_seq)

    def head_peer(step):
        return lax.rem(me_head + step, n_head)

    barrier = pltpu.get_barrier_semaphore()

    @pl.loop(1, n_seq)
    def _(step):
        pl.semaphore_signal(barrier, inc=1, device_id=(seq_peer(step), me_head), device_id_type=MESH)

    @pl.loop(1, n_head)
    def _(step):
        pl.semaphore_signal(barrier, inc=1, device_id=(me_seq, head_peer(step)), device_id_type=MESH)

    factors = [2**level for level in range(1, LEVELS + 1)]
    level_rows = {f: tokens // f for f in factors}
    near_at, far_at, first_row = {}, {}, 0
    for f in reversed(factors):
        near_at[f] = first_row
        far_at[f] = coarse_all + first_row
        first_row += level_rows[f]
    matrix = pool_matrix(factors + [TOP_POOL])
    for side, source in enumerate((k_ref, v_ref)):
        columns = pl.ds(side * width, width)
        held = []
        for chunk in range(tokens // CHUNK):
            pooled = jnp.dot(matrix, source[pl.ds(chunk * CHUNK, CHUNK), :],
                             preferred_element_type=jnp.float32)
            start = 0
            for f in factors:
                size = CHUNK // f
                near[pl.ds(near_at[f] + chunk * size, size), columns] = (
                    pooled[start:start + size].astype(jnp.bfloat16))
                start += size
            held.append(pooled[start:])
        far[pl.ds(pl.multiple_of(me_seq * coarse_rows, coarse_rows), coarse_rows), columns] = (
            jnp.concatenate(held, axis=0).astype(jnp.bfloat16))

    pl.semaphore_wait(barrier, n_seq - 1 + n_head - 1)

    def level_copy(level):
        f = 2**level
        distance = 2 ** (level - 1)
        partner = me_seq + distance * (1 - 2 * lax.rem(me_seq // distance, 2))
        return pltpu.make_async_remote_copy(
            src_ref=near.at[pl.ds(near_at[f], level_rows[f])],
            dst_ref=far.at[pl.ds(far_at[f], level_rows[f])],
            send_sem=level_send.at[level - 1],
            recv_sem=level_recv.at[level - 1],
            device_id=(partner, me_head),
            device_id_type=MESH,
        )

    def coarse_copy(step):
        mine = far.at[pl.ds(pl.multiple_of(me_seq * coarse_rows, coarse_rows), coarse_rows)]
        return pltpu.make_async_remote_copy(
            src_ref=mine,
            dst_ref=mine,
            send_sem=coarse_send.at[step],
            recv_sem=coarse_recv.at[step],
            device_id=(seq_peer(step), me_head),
            device_id_type=MESH,
        )

    @pl.loop(1, n_seq)
    def _(step):
        coarse_copy(step).start()

    level_copies = {level: level_copy(level) for level in range(1, LEVELS + 1)}
    for level in (1, 3, 2):
        level_copies[level].start()

    lane_head = lax.broadcasted_iota(jnp.int32, (1, width), 1) // HEAD_DIM
    scaled_masks = [
        jnp.where(lane_head == h, 1.0 / math.sqrt(HEAD_DIM), 0.0).astype(jnp.bfloat16)
        for h in range(heads)
    ]
    left = lax.broadcasted_iota(jnp.int32, (QUERY_TILE, LANES), 1) < HEAD_DIM

    def attend(tile, keys, values, first, last):
        rows = pl.ds(pl.multiple_of(tile * QUERY_TILE, QUERY_TILE), QUERY_TILE)
        query = q_ref[rows, :]
        ones = jnp.ones((keys.shape[0], LANES), jnp.bfloat16)

        def scores(h):
            return lax.dot_general(query * scaled_masks[h], keys, (((1,), (1,)), ((), ())),
                                   preferred_element_type=jnp.float32)

        ready = scores(0)
        shares = []
        for h in range(heads):
            score = ready
            if h + 1 < heads:
                ready = scores(h + 1)
            highest = jnp.max(score, axis=-1, keepdims=True)
            if not first:
                before = high[h, rows, :]
                highest = jnp.maximum(before[:, :1], highest)
            weights = jnp.exp2((score - highest) * LOG2E).astype(jnp.bfloat16)
            pair = (h // 2) * LANES
            summed = jnp.dot(weights, jnp.concatenate([values[:, pair:pair + LANES], ones], axis=1),
                             preferred_element_type=jnp.float32)
            if not first:
                factor = jnp.exp2((before[:, :1] - highest) * LOG2E)
                summed = summed + acc[h, rows, :] * factor
            if last:
                shares.append(summed[:, :LANES] / summed[:, LANES:])
            else:
                acc[h, rows, :] = summed
                high[h, rows, :] = jnp.broadcast_to(highest, (QUERY_TILE, LANES))
        if last:
            total = jnp.zeros((QUERY_TILE, LANES), jnp.float32)
            for pair in range(heads // 2):
                part = jnp.where(left, shares[2 * pair], shares[2 * pair + 1])
                ctx[rows, pl.ds(pair * LANES, LANES)] = part
                total += part * part
            total = jnp.broadcast_to(jnp.sum(total, axis=-1, keepdims=True), (QUERY_TILE, LANES))
            for piece in range(QUERY_TILE // LANES):
                turned = jnp.transpose(total[piece * LANES:(piece + 1) * LANES])
                squares[0, pl.ds(tile * (QUERY_TILE // LANES) + piece, 1), :] = turned[:1]

    tiles = tokens // QUERY_TILE

    @pl.loop(0, tiles)
    def _(tile):
        block = pl.ds(pl.multiple_of(tile * QUERY_TILE // BLOCK * BLOCK, BLOCK), BLOCK)
        attend(tile, k_ref[block, :], v_ref[block, :], True, False)

    def attend_far(start, size, last):
        @pl.loop(0, tiles)
        def _(tile):
            attend(tile, far[start:start + size, :width], far[start:start + size, width:], False, last)

    @pl.loop(1, n_seq)
    def _(step):
        coarse_copy(step).wait()

    level_copies[3].wait()
    attend_far(0, coarse_all + level_rows[8], False)
    level_copies[2].wait()
    attend_far(far_at[4], level_rows[4], False)
    level_copies[1].wait()
    attend_far(far_at[2], level_rows[2], True)

    square_copies = [
        pltpu.make_async_remote_copy(
            src_ref=squares.at[0],
            dst_ref=squares.at[step],
            send_sem=square_send.at[step],
            recv_sem=square_recv.at[step],
            device_id=(me_seq, head_peer(step)),
            device_id_type=MESH,
        )
        for step in range(1, n_head)
    ]
    for copy in square_copies:
        copy.start()
    for copy in square_copies:
        copy.wait()
    square_total = squares[0]
    for step in range(1, n_head):
        square_total = square_total + squares[step]
    inverse = lax.rsqrt(square_total / (width * n_head) + 1e-6)
    gain = g_ref[...].astype(jnp.float32)
    for piece in range(tokens // LANES):
        rows = pl.ds(piece * LANES, LANES)
        turned = jnp.transpose(jnp.broadcast_to(inverse[piece:piece + 1], (LANES, LANES)))
        for part in range(width // LANES):
            columns = pl.ds(part * LANES, LANES)
            o_ref[rows, columns] = (
                ctx[rows, columns] * turned * gain[:, part * LANES:(part + 1) * LANES]
            ).astype(jnp.bfloat16)


def body(n_seq, n_head, query_rows, key_rows, value_rows, norm_gain):
    tokens, width = query_rows.shape
    heads = width // HEAD_DIM
    level_total = sum(tokens // 2**level for level in range(1, LEVELS + 1))
    coarse_all = tokens // TOP_POOL * n_seq
    keys = BLOCK + level_total + coarse_all
    vmem = pl.BlockSpec(memory_space=pltpu.VMEM)
    dma = pltpu.SemaphoreType.DMA
    return pl.pallas_call(
        functools.partial(kernel, n_seq, n_head),
        out_shape=jax.ShapeDtypeStruct((tokens, width), jnp.bfloat16),
        in_specs=[vmem] * 4,
        out_specs=vmem,
        scratch_shapes=[
            pltpu.VMEM((level_total, 2 * width), jnp.bfloat16),
            pltpu.VMEM((coarse_all + level_total, 2 * width), jnp.bfloat16),
            pltpu.VMEM((heads, tokens, 2 * LANES), jnp.float32),
            pltpu.VMEM((heads, tokens, LANES), jnp.float32),
            pltpu.VMEM((tokens, width), jnp.float32),
            pltpu.VMEM((n_head, tokens // LANES, LANES), jnp.float32),
            dma((LEVELS,)),
            dma((LEVELS,)),
            dma((n_seq,)),
            dma((n_seq,)),
            dma((n_head,)),
            dma((n_head,)),
        ],
        compiler_params=pltpu.CompilerParams(
            collective_id=0, has_side_effects=True, vmem_limit_bytes=56 * 1024 * 1024
        ),
        cost_estimate=pl.CostEstimate(
            flops=4 * tokens * keys * width,
            bytes_accessed=8 * tokens * width,
            transcendentals=tokens * keys * heads,
        ),
    )(query_rows, key_rows, value_rows, norm_gain.reshape(1, width))


def solution(mesh):
    placed = (P("seq", "head"), P("seq", "head"), P("seq", "head"), P("head"))
    return jax.shard_map(
        functools.partial(body, mesh.shape["seq"], mesh.shape["head"]),
        mesh=mesh, in_specs=placed, out_specs=P("seq", "head"), check_vma=False,
    )
```

```python
import functools
import math

import jax
import jax.numpy as jnp
from jax import lax
from jax.experimental import pallas as pl
from jax.experimental.pallas import tpu as pltpu
from jax.sharding import PartitionSpec as P

D = 1024
HEAD_DIM = 64
BLOCK = 1024
LEVELS = 3
TOP_POOL = 32
QUERY_TILE = 512
CHUNK = 256
LANES = 128
LOG2E = math.log2(math.e)
MESH = pl.DeviceIdType.MESH


def pool_matrix(factors):
    pieces = []
    for factor in factors:
        shape = (CHUNK // factor, CHUNK)
        row = lax.broadcasted_iota(jnp.int32, shape, 0)
        window = lax.broadcasted_iota(jnp.int32, shape, 1) // factor
        pieces.append(jnp.where(window == row, 1.0 / factor, 0.0))
    return jnp.concatenate(pieces, axis=0).astype(jnp.bfloat16)


def kernel(n_seq, n_head, q_hbm, k_ref, v_ref, ctx_hbm, inverse_ref,
           q_ref, near, far, acc, high, ctx, squares,
           level_send, level_recv, coarse_send, coarse_recv, square_send, square_recv, q_sem, ctx_sem):
    tokens, width = q_ref.shape
    q_copy = pltpu.make_async_copy(q_hbm, q_ref, q_sem)
    q_copy.start()
    heads = width // HEAD_DIM
    coarse_rows = tokens // TOP_POOL
    coarse_all = coarse_rows * n_seq
    me_seq = lax.axis_index("seq")
    me_head = lax.axis_index("head")

    def seq_peer(step):
        return lax.rem(me_seq + step, n_seq)

    def head_peer(step):
        return lax.rem(me_head + step, n_head)

    barrier = pltpu.get_barrier_semaphore()

    @pl.loop(1, n_seq)
    def _(step):
        pl.semaphore_signal(barrier, inc=1, device_id=(seq_peer(step), me_head), device_id_type=MESH)

    @pl.loop(1, n_head)
    def _(step):
        pl.semaphore_signal(barrier, inc=1, device_id=(me_seq, head_peer(step)), device_id_type=MESH)

    factors = [2**level for level in range(1, LEVELS + 1)]
    level_rows = {f: tokens // f for f in factors}
    near_at, far_at, first_row = {}, {}, 0
    for f in reversed(factors):
        near_at[f] = first_row
        far_at[f] = coarse_all + first_row
        first_row += level_rows[f]
    matrix = pool_matrix(factors + [TOP_POOL])
    for side, source in enumerate((k_ref, v_ref)):
        columns = pl.ds(side * width, width)
        held = []
        for chunk in range(tokens // CHUNK):
            pooled = jnp.dot(matrix, source[pl.ds(chunk * CHUNK, CHUNK), :],
                             preferred_element_type=jnp.float32)
            start = 0
            for f in factors:
                size = CHUNK // f
                near[pl.ds(near_at[f] + chunk * size, size), columns] = (
                    pooled[start:start + size].astype(jnp.bfloat16))
                start += size
            held.append(pooled[start:])
        far[pl.ds(pl.multiple_of(me_seq * coarse_rows, coarse_rows), coarse_rows), columns] = (
            jnp.concatenate(held, axis=0).astype(jnp.bfloat16))

    pl.semaphore_wait(barrier, n_seq - 1 + n_head - 1)

    def level_copy(level):
        f = 2**level
        distance = 2 ** (level - 1)
        partner = me_seq + distance * (1 - 2 * lax.rem(me_seq // distance, 2))
        return pltpu.make_async_remote_copy(
            src_ref=near.at[pl.ds(near_at[f], level_rows[f])],
            dst_ref=far.at[pl.ds(far_at[f], level_rows[f])],
            send_sem=level_send.at[level - 1],
            recv_sem=level_recv.at[level - 1],
            device_id=(partner, me_head),
            device_id_type=MESH,
        )

    def coarse_copy(step):
        mine = far.at[pl.ds(pl.multiple_of(me_seq * coarse_rows, coarse_rows), coarse_rows)]
        return pltpu.make_async_remote_copy(
            src_ref=mine,
            dst_ref=mine,
            send_sem=coarse_send.at[step],
            recv_sem=coarse_recv.at[step],
            device_id=(seq_peer(step), me_head),
            device_id_type=MESH,
        )

    @pl.loop(1, n_seq)
    def _(step):
        coarse_copy(step).start()

    level_copies = {level: level_copy(level) for level in range(1, LEVELS + 1)}
    for level in (1, 3, 2):
        level_copies[level].start()

    lane_head = lax.broadcasted_iota(jnp.int32, (1, width), 1) // HEAD_DIM
    scaled_masks = [
        jnp.where(lane_head == h, 1.0 / math.sqrt(HEAD_DIM), 0.0).astype(jnp.bfloat16)
        for h in range(heads)
    ]
    left = lax.broadcasted_iota(jnp.int32, (QUERY_TILE, LANES), 1) < HEAD_DIM

    def attend(tile, keys, values, first, last):
        rows = pl.ds(pl.multiple_of(tile * QUERY_TILE, QUERY_TILE), QUERY_TILE)
        query = q_ref[rows, :]
        ones = jnp.ones((keys.shape[0], LANES), jnp.bfloat16)

        def scores(h):
            return lax.dot_general(query * scaled_masks[h], keys, (((1,), (1,)), ((), ())),
                                   preferred_element_type=jnp.float32)

        ready = scores(0)
        shares = []
        for h in range(heads):
            score = ready
            if h + 1 < heads:
                ready = scores(h + 1)
            highest = jnp.max(score, axis=-1, keepdims=True)
            if not first:
                before = high[h, rows, :]
                highest = jnp.maximum(before[:, :1], highest)
            weights = jnp.exp2((score - highest) * LOG2E).astype(jnp.bfloat16)
            pair = (h // 2) * LANES
            summed = jnp.dot(weights, jnp.concatenate([values[:, pair:pair + LANES], ones], axis=1),
                             preferred_element_type=jnp.float32)
            if not first:
                factor = jnp.exp2((before[:, :1] - highest) * LOG2E)
                summed = summed + acc[h, rows, :] * factor
            if last:
                shares.append(summed[:, :LANES] / summed[:, LANES:])
            else:
                acc[h, rows, :] = summed
                high[h, rows, :] = jnp.broadcast_to(highest, (QUERY_TILE, LANES))
        if last:
            total = jnp.zeros((QUERY_TILE, LANES), jnp.float32)
            for pair in range(heads // 2):
                part = jnp.where(left, shares[2 * pair], shares[2 * pair + 1])
                ctx[rows, pl.ds(pair * LANES, LANES)] = part
                total += part * part
            total = jnp.broadcast_to(jnp.sum(total, axis=-1, keepdims=True), (QUERY_TILE, LANES))
            for piece in range(QUERY_TILE // LANES):
                turned = jnp.transpose(total[piece * LANES:(piece + 1) * LANES])
                squares[0, pl.ds(tile * (QUERY_TILE // LANES) + piece, 1), :] = turned[:1]

    tiles = tokens // QUERY_TILE

    def ctx_copy(tile):
        rows = pl.ds(pl.multiple_of(tile * QUERY_TILE, QUERY_TILE), QUERY_TILE)
        return pltpu.make_async_copy(ctx.at[rows], ctx_hbm.at[rows], ctx_sem.at[tile])

    q_copy.wait()

    @pl.loop(0, tiles)
    def _(tile):
        block = pl.ds(pl.multiple_of(tile * QUERY_TILE // BLOCK * BLOCK, BLOCK), BLOCK)
        attend(tile, k_ref[block, :], v_ref[block, :], True, False)

    def attend_far(start, size, last):
        @pl.loop(0, tiles)
        def _(tile):
            attend(tile, far[start:start + size, :width], far[start:start + size, width:], False, last)
            if last:
                ctx_copy(tile).start()

    @pl.loop(1, n_seq)
    def _(step):
        coarse_copy(step).wait()

    level_copies[3].wait()
    level_copies[2].wait()
    attend_far(0, coarse_all + level_rows[8] + level_rows[4], False)
    level_copies[1].wait()
    attend_far(far_at[2], level_rows[2], True)

    square_copies = [
        pltpu.make_async_remote_copy(
            src_ref=squares.at[0],
            dst_ref=squares.at[step],
            send_sem=square_send.at[step],
            recv_sem=square_recv.at[step],
            device_id=(me_seq, head_peer(step)),
            device_id_type=MESH,
        )
        for step in range(1, n_head)
    ]
    for copy in square_copies:
        copy.start()
    for copy in square_copies:
        copy.wait()
    square_total = squares[0]
    for step in range(1, n_head):
        square_total = square_total + squares[step]
    inverse_ref[...] = lax.rsqrt(square_total / (width * n_head) + 1e-6)

    @pl.loop(0, tiles)
    def _(tile):
        ctx_copy(tile).wait()


def normalize(ctx_ref, inverse_ref, g_ref, o_ref):
    tokens, width = ctx_ref.shape
    gain = g_ref[...].astype(jnp.float32)
    for piece in range(tokens // LANES):
        rows = pl.ds(piece * LANES, LANES)
        turned = jnp.transpose(jnp.broadcast_to(inverse_ref[piece:piece + 1, :], (LANES, LANES)))
        for part in range(width // LANES):
            columns = pl.ds(part * LANES, LANES)
            o_ref[rows, columns] = (
                ctx_ref[rows, columns] * turned * gain[None, part * LANES:(part + 1) * LANES]
            ).astype(jnp.bfloat16)


def body(n_seq, n_head, query_rows, key_rows, value_rows, norm_gain):
    tokens, width = query_rows.shape
    heads = width // HEAD_DIM
    level_total = sum(tokens // 2**level for level in range(1, LEVELS + 1))
    coarse_all = tokens // TOP_POOL * n_seq
    keys = BLOCK + level_total + coarse_all
    vmem = pl.BlockSpec(memory_space=pltpu.VMEM)
    dma = pltpu.SemaphoreType.DMA
    context, inverse = pl.pallas_call(
        functools.partial(kernel, n_seq, n_head),
        out_shape=[
            jax.ShapeDtypeStruct((tokens, width), jnp.float32),
            jax.ShapeDtypeStruct((tokens // LANES, LANES), jnp.float32),
        ],
        in_specs=[pl.BlockSpec(memory_space=pl.ANY), vmem, vmem],
        out_specs=[pl.BlockSpec(memory_space=pl.ANY), vmem],
        scratch_shapes=[
            pltpu.VMEM((tokens, width), jnp.bfloat16),
            pltpu.VMEM((level_total, 2 * width), jnp.bfloat16),
            pltpu.VMEM((coarse_all + level_total, 2 * width), jnp.bfloat16),
            pltpu.VMEM((heads, tokens, 2 * LANES), jnp.float32),
            pltpu.VMEM((heads, tokens, LANES), jnp.float32),
            pltpu.VMEM((tokens, width), jnp.float32),
            pltpu.VMEM((n_head, tokens // LANES, LANES), jnp.float32),
            dma((LEVELS,)),
            dma((LEVELS,)),
            dma((n_seq,)),
            dma((n_seq,)),
            dma((n_head,)),
            dma((n_head,)),
            dma,
            dma((tokens // QUERY_TILE,)),
        ],
        compiler_params=pltpu.CompilerParams(
            collective_id=0, has_side_effects=True, vmem_limit_bytes=56 * 1024 * 1024
        ),
        cost_estimate=pl.CostEstimate(
            flops=4 * tokens * keys * width,
            bytes_accessed=8 * tokens * width,
            transcendentals=tokens * keys * heads,
        ),
    )(query_rows, key_rows, value_rows)
    return pl.pallas_call(
        normalize,
        out_shape=jax.ShapeDtypeStruct((tokens, width), jnp.bfloat16),
        in_specs=[vmem] * 3,
        out_specs=vmem,
        compiler_params=pltpu.CompilerParams(vmem_limit_bytes=16 * 1024 * 1024),
    )(context, inverse, norm_gain)


def solution(mesh):
    placed = (P("seq", "head"), P("seq", "head"), P("seq", "head"), P("head"))
    return jax.shard_map(
        functools.partial(body, mesh.shape["seq"], mesh.shape["head"]),
        mesh=mesh, in_specs=placed, out_specs=P("seq", "head"), check_vma=False,
    )
```

```python
import functools
import math

import jax
import jax.numpy as jnp
from jax import lax
from jax.experimental import pallas as pl
from jax.experimental.pallas import tpu as pltpu
from jax.sharding import PartitionSpec as P

D = 1024
HEAD_DIM = 64
BLOCK = 1024
LEVELS = 3
TOP_POOL = 32
QUERY_TILE = 512
WIDE_TILE = 1024
CHUNK = 256
LANES = 128
LOG2E = math.log2(math.e)
MESH = pl.DeviceIdType.MESH


def pool_matrix(factors):
    pieces = []
    for factor in factors:
        shape = (CHUNK // factor, CHUNK)
        row = lax.broadcasted_iota(jnp.int32, shape, 0)
        window = lax.broadcasted_iota(jnp.int32, shape, 1) // factor
        pieces.append(jnp.where(window == row, 1.0 / factor, 0.0))
    return jnp.concatenate(pieces, axis=0).astype(jnp.bfloat16)


def kernel(n_seq, n_head, q_hbm, k_ref, v_ref, ctx_hbm, inverse_ref,
           q_ref, near, far, acc, high, ctx, squares,
           level_send, level_recv, coarse_send, coarse_recv, square_send, square_recv, q_sem, ctx_sem):
    tokens, width = q_ref.shape
    q_copy = pltpu.make_async_copy(q_hbm, q_ref, q_sem)
    q_copy.start()
    heads = width // HEAD_DIM
    coarse_rows = tokens // TOP_POOL
    coarse_all = coarse_rows * n_seq
    me_seq = lax.axis_index("seq")
    me_head = lax.axis_index("head")

    def seq_peer(step):
        return lax.rem(me_seq + step, n_seq)

    def head_peer(step):
        return lax.rem(me_head + step, n_head)

    barrier = pltpu.get_barrier_semaphore()

    @pl.loop(1, n_seq)
    def _(step):
        pl.semaphore_signal(barrier, inc=1, device_id=(seq_peer(step), me_head), device_id_type=MESH)

    @pl.loop(1, n_head)
    def _(step):
        pl.semaphore_signal(barrier, inc=1, device_id=(me_seq, head_peer(step)), device_id_type=MESH)

    factors = [2**level for level in range(1, LEVELS + 1)]
    level_rows = {f: tokens // f for f in factors}
    level_at, first_row = {}, 0
    for f in reversed(factors):
        level_at[f] = first_row
        first_row += level_rows[f]
    coarse_at = first_row
    my_coarse = pl.ds(pl.multiple_of(coarse_at + me_seq * coarse_rows, coarse_rows), coarse_rows)
    matrix = pool_matrix(factors + [TOP_POOL])

    def pool(plane, source):
        held = []
        for chunk in range(tokens // CHUNK):
            pooled = jnp.dot(matrix, source[pl.ds(chunk * CHUNK, CHUNK), :],
                             preferred_element_type=jnp.float32)
            start = 0
            for f in factors:
                size = CHUNK // f
                near[plane, pl.ds(level_at[f] + chunk * size, size), :] = (
                    pooled[start:start + size].astype(jnp.bfloat16))
                start += size
            held.append(pooled[start:])
        far[plane, my_coarse, :] = jnp.concatenate(held, axis=0).astype(jnp.bfloat16)

    def level_copy(level, plane):
        f = 2**level
        distance = 2 ** (level - 1)
        partner = me_seq + distance * (1 - 2 * lax.rem(me_seq // distance, 2))
        rows = pl.ds(level_at[f], level_rows[f])
        return pltpu.make_async_remote_copy(
            src_ref=near.at[plane, rows],
            dst_ref=far.at[plane, rows],
            send_sem=level_send.at[level - 1, plane],
            recv_sem=level_recv.at[level - 1, plane],
            device_id=(partner, me_head),
            device_id_type=MESH,
        )

    def coarse_copy(step):
        mine = far.at[:, my_coarse]
        return pltpu.make_async_remote_copy(
            src_ref=mine,
            dst_ref=mine,
            send_sem=coarse_send.at[step],
            recv_sem=coarse_recv.at[step],
            device_id=(seq_peer(step), me_head),
            device_id_type=MESH,
        )

    pool(0, k_ref)
    pl.semaphore_wait(barrier, n_seq - 1 + n_head - 1)
    level_copies = {
        (level, plane): level_copy(level, plane)
        for level in range(1, LEVELS + 1) for plane in range(2)
    }
    for level in (1, 2, 3):
        level_copies[level, 0].start()
    pool(1, v_ref)
    for level in (1, 2, 3):
        level_copies[level, 1].start()

    lane_head = lax.broadcasted_iota(jnp.int32, (1, width), 1) // HEAD_DIM
    scaled_masks = [
        jnp.where(lane_head == h, 1.0 / math.sqrt(HEAD_DIM), 0.0).astype(jnp.bfloat16)
        for h in range(heads)
    ]
    left = lax.broadcasted_iota(jnp.int32, (1, LANES), 1) < HEAD_DIM

    def attend(tile, size, keys, values, first, last):
        rows = pl.ds(pl.multiple_of(tile * size, size), size)
        query = q_ref[rows, :]
        ones = jnp.ones((keys.shape[0], LANES), jnp.bfloat16)

        def scores(h):
            return lax.dot_general(query * scaled_masks[h], keys, (((1,), (1,)), ((), ())),
                                   preferred_element_type=jnp.float32)

        ready = scores(0)
        shares = []
        for h in range(heads):
            score = ready
            if h + 1 < heads:
                ready = scores(h + 1)
            highest = jnp.max(score, axis=-1, keepdims=True)
            if not first:
                before = high[h, rows, :]
                highest = jnp.maximum(before[:, :1], highest)
            weights = jnp.exp2((score - highest) * LOG2E).astype(jnp.bfloat16)
            pair = (h // 2) * LANES
            summed = jnp.dot(weights, jnp.concatenate([values[:, pair:pair + LANES], ones], axis=1),
                             preferred_element_type=jnp.float32)
            if not first:
                factor = jnp.exp2((before[:, :1] - highest) * LOG2E)
                summed = summed + acc[h, rows, :] * factor
            if last:
                shares.append(summed[:, :LANES] / summed[:, LANES:])
            else:
                acc[h, rows, :] = summed
                high[h, rows, :] = jnp.broadcast_to(highest, (size, LANES))
        if last:
            total = jnp.zeros((size, LANES), jnp.float32)
            for pair in range(heads // 2):
                part = jnp.where(left, shares[2 * pair], shares[2 * pair + 1])
                ctx[rows, pl.ds(pair * LANES, LANES)] = part
                total += part * part
            total = jnp.broadcast_to(jnp.sum(total, axis=-1, keepdims=True), (size, LANES))
            for piece in range(size // LANES):
                turned = jnp.transpose(total[piece * LANES:(piece + 1) * LANES])
                squares[0, pl.ds(tile * (size // LANES) + piece, 1), :] = turned[:1]

    tiles = tokens // QUERY_TILE

    def ctx_copy(tile):
        rows = pl.ds(pl.multiple_of(tile * QUERY_TILE, QUERY_TILE), QUERY_TILE)
        return pltpu.make_async_copy(ctx.at[rows], ctx_hbm.at[rows], ctx_sem.at[tile])

    q_copy.wait()

    @pl.loop(0, tokens // WIDE_TILE)
    def _(tile):
        block = pl.ds(pl.multiple_of(tile * WIDE_TILE // BLOCK * BLOCK, BLOCK), BLOCK)
        attend(tile, WIDE_TILE, k_ref[block, :], v_ref[block, :], True, False)

    @pl.loop(1, n_seq)
    def _(step):
        coarse_copy(step).start()

    for level in (3, 2):
        for plane in range(2):
            level_copies[level, plane].wait()
    middle = pl.ds(0, level_at[2])

    @pl.loop(0, tokens // WIDE_TILE)
    def _(tile):
        attend(tile, WIDE_TILE, far[0, middle, :], far[1, middle, :], False, False)

    for plane in range(2):
        level_copies[1, plane].wait()

    @pl.loop(1, n_seq)
    def _(step):
        coarse_copy(step).wait()

    rest = pl.ds(level_at[2], level_rows[2] + coarse_all)

    @pl.loop(0, tiles)
    def _(tile):
        attend(tile, QUERY_TILE, far[0, rest, :], far[1, rest, :], False, True)
        ctx_copy(tile).start()

    square_copies = [
        pltpu.make_async_remote_copy(
            src_ref=squares.at[0],
            dst_ref=squares.at[step],
            send_sem=square_send.at[step],
            recv_sem=square_recv.at[step],
            device_id=(me_seq, head_peer(step)),
            device_id_type=MESH,
        )
        for step in range(1, n_head)
    ]
    for copy in square_copies:
        copy.start()
    for copy in square_copies:
        copy.wait()
    square_total = squares[0]
    for step in range(1, n_head):
        square_total = square_total + squares[step]
    inverse_ref[...] = lax.rsqrt(square_total / (width * n_head) + 1e-6)

    @pl.loop(0, tiles)
    def _(tile):
        ctx_copy(tile).wait()


def normalize(ctx_ref, inverse_ref, g_ref, o_ref):
    size, width = ctx_ref.shape
    gain = g_ref[...].astype(jnp.float32)
    first = pl.program_id(0) * (size // LANES)
    for piece in range(size // LANES):
        rows = pl.ds(piece * LANES, LANES)
        inverse = inverse_ref[pl.ds(first + piece, 1), :]
        turned = jnp.transpose(jnp.broadcast_to(inverse, (LANES, LANES)))
        for part in range(width // LANES):
            columns = pl.ds(part * LANES, LANES)
            o_ref[rows, columns] = (
                ctx_ref[rows, columns] * turned * gain[None, part * LANES:(part + 1) * LANES]
            ).astype(jnp.bfloat16)


def body(n_seq, n_head, query_rows, key_rows, value_rows, norm_gain):
    tokens, width = query_rows.shape
    heads = width // HEAD_DIM
    level_total = sum(tokens // 2**level for level in range(1, LEVELS + 1))
    coarse_all = tokens // TOP_POOL * n_seq
    keys = BLOCK + level_total + coarse_all
    vmem = pl.BlockSpec(memory_space=pltpu.VMEM)
    dma = pltpu.SemaphoreType.DMA
    context, inverse = pl.pallas_call(
        functools.partial(kernel, n_seq, n_head),
        out_shape=[
            jax.ShapeDtypeStruct((tokens, width), jnp.float32),
            jax.ShapeDtypeStruct((tokens // LANES, LANES), jnp.float32),
        ],
        in_specs=[pl.BlockSpec(memory_space=pl.ANY), vmem, vmem],
        out_specs=[pl.BlockSpec(memory_space=pl.ANY), vmem],
        scratch_shapes=[
            pltpu.VMEM((tokens, width), jnp.bfloat16),
            pltpu.VMEM((2, level_total, width), jnp.bfloat16),
            pltpu.VMEM((2, level_total + coarse_all, width), jnp.bfloat16),
            pltpu.VMEM((heads, tokens, 2 * LANES), jnp.float32),
            pltpu.VMEM((heads, tokens, LANES), jnp.float32),
            pltpu.VMEM((tokens, width), jnp.float32),
            pltpu.VMEM((n_head, tokens // LANES, LANES), jnp.float32),
            dma((LEVELS, 2)),
            dma((LEVELS, 2)),
            dma((n_seq,)),
            dma((n_seq,)),
            dma((n_head,)),
            dma((n_head,)),
            dma,
            dma((tokens // QUERY_TILE,)),
        ],
        compiler_params=pltpu.CompilerParams(
            collective_id=0, has_side_effects=True, vmem_limit_bytes=56 * 1024 * 1024
        ),
        cost_estimate=pl.CostEstimate(
            flops=4 * tokens * keys * width,
            bytes_accessed=8 * tokens * width,
            transcendentals=tokens * keys * heads,
        ),
    )(query_rows, key_rows, value_rows)
    return pl.pallas_call(
        normalize,
        out_shape=jax.ShapeDtypeStruct((tokens, width), jnp.bfloat16),
        grid=(tokens // QUERY_TILE,),
        in_specs=[pl.BlockSpec((QUERY_TILE, width), lambda i: (i, 0)), vmem, vmem],
        out_specs=pl.BlockSpec((QUERY_TILE, width), lambda i: (i, 0)),
        compiler_params=pltpu.CompilerParams(vmem_limit_bytes=60 * 1024 * 1024),
    )(context, inverse, norm_gain)


def solution(mesh):
    placed = (P("seq", "head"), P("seq", "head"), P("seq", "head"), P("head"))
    return jax.shard_map(
        functools.partial(body, mesh.shape["seq"], mesh.shape["head"]),
        mesh=mesh, in_specs=placed, out_specs=P("seq", "head"), check_vma=False,
    )
```

```python
import functools
import math

import jax
import jax.numpy as jnp
from jax import lax
from jax.experimental import pallas as pl
from jax.experimental.pallas import tpu as pltpu
from jax.sharding import PartitionSpec as P

D = 1024
HEAD_DIM = 64
BLOCK = 1024
LEVELS = 3
TOP_POOL = 32
QUERY_TILE = 512
WIDE_TILE = 1024
CHUNK = 256
LANES = 128
LOG2E = math.log2(math.e)
MESH = pl.DeviceIdType.MESH


def pool_matrix(factors):
    pieces = []
    for factor in factors:
        shape = (CHUNK // factor, CHUNK)
        row = lax.broadcasted_iota(jnp.int32, shape, 0)
        window = lax.broadcasted_iota(jnp.int32, shape, 1) // factor
        pieces.append(jnp.where(window == row, 1.0 / factor, 0.0))
    return jnp.concatenate(pieces, axis=0).astype(jnp.bfloat16)


def kernel(n_seq, n_head, q_hbm, k_ref, v_ref, ctx_hbm, inverse_ref,
           q_ref, near, far, acc, high, ctx, squares,
           level_send, level_recv, coarse_send, coarse_recv, square_send, square_recv, q_sem, ctx_sem):
    tokens, width = q_ref.shape
    q_copy = pltpu.make_async_copy(q_hbm, q_ref, q_sem)
    q_copy.start()
    heads = width // HEAD_DIM
    coarse_rows = tokens // TOP_POOL
    coarse_all = coarse_rows * n_seq
    me_seq = lax.axis_index("seq")
    me_head = lax.axis_index("head")

    def seq_peer(step):
        return lax.rem(me_seq + step, n_seq)

    def head_peer(step):
        return lax.rem(me_head + step, n_head)

    barrier = pltpu.get_barrier_semaphore()

    @pl.loop(1, n_seq)
    def _(step):
        pl.semaphore_signal(barrier, inc=1, device_id=(seq_peer(step), me_head), device_id_type=MESH)

    @pl.loop(1, n_head)
    def _(step):
        pl.semaphore_signal(barrier, inc=1, device_id=(me_seq, head_peer(step)), device_id_type=MESH)

    factors = [2**level for level in range(1, LEVELS + 1)]
    level_rows = {f: tokens // f for f in factors}
    level_at, first_row = {}, 0
    for f in reversed(factors):
        level_at[f] = first_row
        first_row += level_rows[f]
    coarse_at = first_row
    my_coarse = pl.ds(pl.multiple_of(coarse_at + me_seq * coarse_rows, coarse_rows), coarse_rows)
    matrix = pool_matrix(factors + [TOP_POOL])

    def pool(plane, source):
        held = []
        for chunk in range(tokens // CHUNK):
            pooled = jnp.dot(matrix, source[pl.ds(chunk * CHUNK, CHUNK), :],
                             preferred_element_type=jnp.float32)
            start = 0
            for f in factors:
                size = CHUNK // f
                near[plane, pl.ds(level_at[f] + chunk * size, size), :] = (
                    pooled[start:start + size].astype(jnp.bfloat16))
                start += size
            held.append(pooled[start:])
        far[plane, my_coarse, :] = jnp.concatenate(held, axis=0).astype(jnp.bfloat16)

    def level_copy(level, plane):
        f = 2**level
        distance = 2 ** (level - 1)
        partner = me_seq + distance * (1 - 2 * lax.rem(me_seq // distance, 2))
        rows = pl.ds(level_at[f], level_rows[f])
        return pltpu.make_async_remote_copy(
            src_ref=near.at[plane, rows],
            dst_ref=far.at[plane, rows],
            send_sem=level_send.at[level - 1, plane],
            recv_sem=level_recv.at[level - 1, plane],
            device_id=(partner, me_head),
            device_id_type=MESH,
        )

    def coarse_copy(step):
        mine = far.at[:, my_coarse]
        return pltpu.make_async_remote_copy(
            src_ref=mine,
            dst_ref=mine,
            send_sem=coarse_send.at[step],
            recv_sem=coarse_recv.at[step],
            device_id=(seq_peer(step), me_head),
            device_id_type=MESH,
        )

    pool(0, k_ref)
    pl.semaphore_wait(barrier, n_seq - 1 + n_head - 1)
    level_copies = {
        (level, plane): level_copy(level, plane)
        for level in range(1, LEVELS + 1) for plane in range(2)
    }
    for level in (1, 2, 3):
        level_copies[level, 0].start()
    pool(1, v_ref)
    for level in (1, 2, 3):
        level_copies[level, 1].start()

    @pl.loop(1, n_seq)
    def _(step):
        coarse_copy(step).start()

    lane_head = lax.broadcasted_iota(jnp.int32, (1, width), 1) // HEAD_DIM
    scaled_masks = [
        jnp.where(lane_head == h, 1.0 / math.sqrt(HEAD_DIM), 0.0).astype(jnp.bfloat16)
        for h in range(heads)
    ]
    left = lax.broadcasted_iota(jnp.int32, (1, LANES), 1) < HEAD_DIM

    def attend(tile, size, keys, values, first, last):
        rows = pl.ds(pl.multiple_of(tile * size, size), size)
        query = q_ref[rows, :]
        ones = jnp.ones((keys.shape[0], LANES), jnp.bfloat16)

        def scores(h):
            return lax.dot_general(query * scaled_masks[h], keys, (((1,), (1,)), ((), ())),
                                   preferred_element_type=jnp.float32)

        ready = scores(0)
        shares = []
        for h in range(heads):
            score = ready
            if h + 1 < heads:
                ready = scores(h + 1)
            highest = jnp.max(score, axis=-1, keepdims=True)
            if not first:
                before = high[h, rows, :]
                highest = jnp.maximum(before[:, :1], highest)
            weights = jnp.exp2((score - highest) * LOG2E).astype(jnp.bfloat16)
            pair = (h // 2) * LANES
            summed = jnp.dot(weights, jnp.concatenate([values[:, pair:pair + LANES], ones], axis=1),
                             preferred_element_type=jnp.float32)
            if not first:
                factor = jnp.exp2((before[:, :1] - highest) * LOG2E)
                summed = summed + acc[h, rows, :] * factor
            if last:
                shares.append(summed[:, :LANES] / summed[:, LANES:])
            else:
                acc[h, rows, :] = summed
                high[h, rows, :] = jnp.broadcast_to(highest, (size, LANES))
        if last:
            total = jnp.zeros((size, LANES), jnp.float32)
            for pair in range(heads // 2):
                part = jnp.where(left, shares[2 * pair], shares[2 * pair + 1])
                ctx[rows, pl.ds(pair * LANES, LANES)] = part
                total += part * part
            total = jnp.broadcast_to(jnp.sum(total, axis=-1, keepdims=True), (size, LANES))
            for piece in range(size // LANES):
                turned = jnp.transpose(total[piece * LANES:(piece + 1) * LANES])
                squares[0, pl.ds(tile * (size // LANES) + piece, 1), :] = turned[:1]

    tiles = tokens // QUERY_TILE

    def ctx_copy(tile):
        rows = pl.ds(pl.multiple_of(tile * QUERY_TILE, QUERY_TILE), QUERY_TILE)
        return pltpu.make_async_copy(ctx.at[rows], ctx_hbm.at[rows], ctx_sem.at[tile])

    q_copy.wait()

    @pl.loop(0, tokens // WIDE_TILE)
    def _(tile):
        block = pl.ds(pl.multiple_of(tile * WIDE_TILE // BLOCK * BLOCK, BLOCK), BLOCK)
        attend(tile, WIDE_TILE, k_ref[block, :], v_ref[block, :], True, False)

    for level in (3, 2):
        for plane in range(2):
            level_copies[level, plane].wait()
    middle = pl.ds(0, level_at[2])

    @pl.loop(0, tokens // WIDE_TILE)
    def _(tile):
        attend(tile, WIDE_TILE, far[0, middle, :], far[1, middle, :], False, False)

    for plane in range(2):
        level_copies[1, plane].wait()

    @pl.loop(1, n_seq)
    def _(step):
        coarse_copy(step).wait()

    rest = pl.ds(level_at[2], level_rows[2] + coarse_all)

    @pl.loop(0, tiles)
    def _(tile):
        attend(tile, QUERY_TILE, far[0, rest, :], far[1, rest, :], False, True)
        ctx_copy(tile).start()

    square_copies = [
        pltpu.make_async_remote_copy(
            src_ref=squares.at[0],
            dst_ref=squares.at[step],
            send_sem=square_send.at[step],
            recv_sem=square_recv.at[step],
            device_id=(me_seq, head_peer(step)),
            device_id_type=MESH,
        )
        for step in range(1, n_head)
    ]
    for copy in square_copies:
        copy.start()
    for copy in square_copies:
        copy.wait()
    square_total = squares[0]
    for step in range(1, n_head):
        square_total = square_total + squares[step]
    inverse_ref[...] = lax.rsqrt(square_total / (width * n_head) + 1e-6)

    @pl.loop(0, tiles)
    def _(tile):
        ctx_copy(tile).wait()


def normalize(ctx_ref, inverse_ref, g_ref, o_ref):
    tokens, width = ctx_ref.shape
    gain = g_ref[...].astype(jnp.float32)
    for piece in range(tokens // LANES):
        rows = pl.ds(piece * LANES, LANES)
        turned = jnp.transpose(jnp.broadcast_to(inverse_ref[piece:piece + 1, :], (LANES, LANES)))
        for part in range(width // LANES):
            columns = pl.ds(part * LANES, LANES)
            o_ref[rows, columns] = (
                ctx_ref[rows, columns] * turned * gain[None, part * LANES:(part + 1) * LANES]
            ).astype(jnp.bfloat16)


def body(n_seq, n_head, query_rows, key_rows, value_rows, norm_gain):
    tokens, width = query_rows.shape
    heads = width // HEAD_DIM
    level_total = sum(tokens // 2**level for level in range(1, LEVELS + 1))
    coarse_all = tokens // TOP_POOL * n_seq
    keys = BLOCK + level_total + coarse_all
    vmem = pl.BlockSpec(memory_space=pltpu.VMEM)
    dma = pltpu.SemaphoreType.DMA
    context, inverse = pl.pallas_call(
        functools.partial(kernel, n_seq, n_head),
        out_shape=[
            jax.ShapeDtypeStruct((tokens, width), jnp.float32),
            jax.ShapeDtypeStruct((tokens // LANES, LANES), jnp.float32),
        ],
        in_specs=[pl.BlockSpec(memory_space=pl.ANY), vmem, vmem],
        out_specs=[pl.BlockSpec(memory_space=pl.ANY), vmem],
        scratch_shapes=[
            pltpu.VMEM((tokens, width), jnp.bfloat16),
            pltpu.VMEM((2, level_total, width), jnp.bfloat16),
            pltpu.VMEM((2, level_total + coarse_all, width), jnp.bfloat16),
            pltpu.VMEM((heads, tokens, 2 * LANES), jnp.float32),
            pltpu.VMEM((heads, tokens, LANES), jnp.float32),
            pltpu.VMEM((tokens, width), jnp.float32),
            pltpu.VMEM((n_head, tokens // LANES, LANES), jnp.float32),
            dma((LEVELS, 2)),
            dma((LEVELS, 2)),
            dma((n_seq,)),
            dma((n_seq,)),
            dma((n_head,)),
            dma((n_head,)),
            dma,
            dma((tokens // QUERY_TILE,)),
        ],
        compiler_params=pltpu.CompilerParams(
            collective_id=0, has_side_effects=True, vmem_limit_bytes=56 * 1024 * 1024
        ),
        cost_estimate=pl.CostEstimate(
            flops=4 * tokens * keys * width,
            bytes_accessed=8 * tokens * width,
            transcendentals=tokens * keys * heads,
        ),
    )(query_rows, key_rows, value_rows)
    return pl.pallas_call(
        normalize,
        out_shape=jax.ShapeDtypeStruct((tokens, width), jnp.bfloat16),
        in_specs=[vmem] * 3,
        out_specs=vmem,
        compiler_params=pltpu.CompilerParams(vmem_limit_bytes=16 * 1024 * 1024),
    )(context, inverse, norm_gain)


def solution(mesh):
    placed = (P("seq", "head"), P("seq", "head"), P("seq", "head"), P("head"))
    return jax.shard_map(
        functools.partial(body, mesh.shape["seq"], mesh.shape["head"]),
        mesh=mesh, in_specs=placed, out_specs=P("seq", "head"), check_vma=False,
    )
```

```python
import functools
import math

import jax
import jax.numpy as jnp
from jax import lax
from jax.experimental import pallas as pl
from jax.experimental.pallas import tpu as pltpu
from jax.sharding import PartitionSpec as P

D = 1024
HEAD_DIM = 64
BLOCK = 1024
LEVELS = 3
TOP_POOL = 32
QUERY_TILE = 512
CHUNK = 256
LANES = 128
LOG2E = math.log2(math.e)
MESH = pl.DeviceIdType.MESH


def pool_matrix(factors):
    pieces = []
    for factor in factors:
        shape = (CHUNK // factor, CHUNK)
        row = lax.broadcasted_iota(jnp.int32, shape, 0)
        window = lax.broadcasted_iota(jnp.int32, shape, 1) // factor
        pieces.append(jnp.where(window == row, 1.0 / factor, 0.0))
    return jnp.concatenate(pieces, axis=0).astype(jnp.bfloat16)


def kernel(n_seq, n_head, q_hbm, k_ref, v_ref, ctx_hbm, inverse_ref,
           q_ref, near, far, acc, high, ctx, squares,
           level_send, level_recv, coarse_send, coarse_recv, square_send, square_recv, q_sem, ctx_sem):
    tokens, width = q_ref.shape
    q_copy = pltpu.make_async_copy(q_hbm, q_ref, q_sem)
    q_copy.start()
    heads = width // HEAD_DIM
    coarse_rows = tokens // TOP_POOL
    coarse_all = coarse_rows * n_seq
    me_seq = lax.axis_index("seq")
    me_head = lax.axis_index("head")

    def seq_peer(step):
        return lax.rem(me_seq + step, n_seq)

    def head_peer(step):
        return lax.rem(me_head + step, n_head)

    barrier = pltpu.get_barrier_semaphore()

    @pl.loop(1, n_seq)
    def _(step):
        pl.semaphore_signal(barrier, inc=1, device_id=(seq_peer(step), me_head), device_id_type=MESH)

    @pl.loop(1, n_head)
    def _(step):
        pl.semaphore_signal(barrier, inc=1, device_id=(me_seq, head_peer(step)), device_id_type=MESH)

    factors = [2**level for level in range(1, LEVELS + 1)]
    level_rows = {f: tokens // f for f in factors}
    near_at, far_at, first_row = {}, {}, 0
    for f in reversed(factors):
        near_at[f] = first_row
        far_at[f] = coarse_all + first_row
        first_row += level_rows[f]
    matrix = pool_matrix(factors + [TOP_POOL])
    for side, source in enumerate((k_ref, v_ref)):
        columns = pl.ds(side * width, width)
        held = []
        for chunk in range(tokens // CHUNK):
            pooled = jnp.dot(matrix, source[pl.ds(chunk * CHUNK, CHUNK), :],
                             preferred_element_type=jnp.float32)
            start = 0
            for f in factors:
                size = CHUNK // f
                near[pl.ds(near_at[f] + chunk * size, size), columns] = (
                    pooled[start:start + size].astype(jnp.bfloat16))
                start += size
            held.append(pooled[start:])
        far[pl.ds(pl.multiple_of(me_seq * coarse_rows, coarse_rows), coarse_rows), columns] = (
            jnp.concatenate(held, axis=0).astype(jnp.bfloat16))

    pl.semaphore_wait(barrier, n_seq - 1 + n_head - 1)

    def level_copy(level, half=0):
        f = 2**level
        size = level_rows[f] // 2 if level == 1 else level_rows[f]
        slot = half * LEVELS + level - 1 if level == 1 else level - 1
        distance = 2 ** (level - 1)
        partner = me_seq + distance * (1 - 2 * lax.rem(me_seq // distance, 2))
        return pltpu.make_async_remote_copy(
            src_ref=near.at[pl.ds(near_at[f] + half * size, size)],
            dst_ref=far.at[pl.ds(far_at[f] + half * size, size)],
            send_sem=level_send.at[slot],
            recv_sem=level_recv.at[slot],
            device_id=(partner, me_head),
            device_id_type=MESH,
        )

    def coarse_copy(step):
        mine = far.at[pl.ds(pl.multiple_of(me_seq * coarse_rows, coarse_rows), coarse_rows)]
        return pltpu.make_async_remote_copy(
            src_ref=mine,
            dst_ref=mine,
            send_sem=coarse_send.at[step],
            recv_sem=coarse_recv.at[step],
            device_id=(seq_peer(step), me_head),
            device_id_type=MESH,
        )

    level_copies = {level: level_copy(level) for level in range(1, LEVELS + 1)}
    later_half = level_copy(1, 1)
    level_copies[1].start()

    @pl.loop(1, n_seq)
    def _(step):
        coarse_copy(step).start()

    for level in (3, 2):
        level_copies[level].start()
    later_half.start()

    lane_head = lax.broadcasted_iota(jnp.int32, (1, width), 1) // HEAD_DIM
    scaled_masks = [
        jnp.where(lane_head == h, 1.0 / math.sqrt(HEAD_DIM), 0.0).astype(jnp.bfloat16)
        for h in range(heads)
    ]
    left = lax.broadcasted_iota(jnp.int32, (QUERY_TILE, LANES), 1) < HEAD_DIM

    def attend(tile, keys, values, first, last):
        rows = pl.ds(pl.multiple_of(tile * QUERY_TILE, QUERY_TILE), QUERY_TILE)
        query = q_ref[rows, :]
        ones = jnp.ones((keys.shape[0], LANES), jnp.bfloat16)

        def scores(h):
            return lax.dot_general(query * scaled_masks[h], keys, (((1,), (1,)), ((), ())),
                                   preferred_element_type=jnp.float32)

        ready = scores(0)
        shares = []
        for h in range(heads):
            score = ready
            if h + 1 < heads:
                ready = scores(h + 1)
            highest = jnp.max(score, axis=-1, keepdims=True)
            if not first:
                before = high[h, rows, :]
                highest = jnp.maximum(before[:, :1], highest)
            weights = jnp.exp2((score - highest) * LOG2E).astype(jnp.bfloat16)
            pair = (h // 2) * LANES
            summed = jnp.dot(weights, jnp.concatenate([values[:, pair:pair + LANES], ones], axis=1),
                             preferred_element_type=jnp.float32)
            if not first:
                factor = jnp.exp2((before[:, :1] - highest) * LOG2E)
                summed = summed + acc[h, rows, :] * factor
            if last:
                shares.append(summed[:, :LANES] / summed[:, LANES:])
            else:
                acc[h, rows, :] = summed
                high[h, rows, :] = jnp.broadcast_to(highest, (QUERY_TILE, LANES))
        if last:
            total = jnp.zeros((QUERY_TILE, LANES), jnp.float32)
            for pair in range(heads // 2):
                part = jnp.where(left, shares[2 * pair], shares[2 * pair + 1])
                ctx[rows, pl.ds(pair * LANES, LANES)] = part
                total += part * part
            total = jnp.broadcast_to(jnp.sum(total, axis=-1, keepdims=True), (QUERY_TILE, LANES))
            for piece in range(QUERY_TILE // LANES):
                turned = jnp.transpose(total[piece * LANES:(piece + 1) * LANES])
                squares[0, pl.ds(tile * (QUERY_TILE // LANES) + piece, 1), :] = turned[:1]

    tiles = tokens // QUERY_TILE

    def ctx_copy(tile):
        rows = pl.ds(pl.multiple_of(tile * QUERY_TILE, QUERY_TILE), QUERY_TILE)
        return pltpu.make_async_copy(ctx.at[rows], ctx_hbm.at[rows], ctx_sem.at[tile])

    q_copy.wait()

    @pl.loop(0, tiles)
    def _(tile):
        block = pl.ds(pl.multiple_of(tile * QUERY_TILE // BLOCK * BLOCK, BLOCK), BLOCK)
        attend(tile, k_ref[block, :], v_ref[block, :], True, False)

    def attend_far(start, size, last):
        @pl.loop(0, tiles)
        def _(tile):
            attend(tile, far[start:start + size, :width], far[start:start + size, width:], False, last)
            if last:
                ctx_copy(tile).start()

    @pl.loop(1, n_seq)
    def _(step):
        coarse_copy(step).wait()

    level_copies[3].wait()
    level_copies[2].wait()
    attend_far(0, coarse_all + level_rows[8] + level_rows[4], False)
    level_copies[1].wait()
    attend_far(far_at[2], level_rows[2] // 2, False)
    later_half.wait()
    attend_far(far_at[2] + level_rows[2] // 2, level_rows[2] // 2, True)

    square_copies = [
        pltpu.make_async_remote_copy(
            src_ref=squares.at[0],
            dst_ref=squares.at[step],
            send_sem=square_send.at[step],
            recv_sem=square_recv.at[step],
            device_id=(me_seq, head_peer(step)),
            device_id_type=MESH,
        )
        for step in range(1, n_head)
    ]
    for copy in square_copies:
        copy.start()
    for copy in square_copies:
        copy.wait()
    square_total = squares[0]
    for step in range(1, n_head):
        square_total = square_total + squares[step]
    inverse_ref[...] = lax.rsqrt(square_total / (width * n_head) + 1e-6)

    @pl.loop(0, tiles)
    def _(tile):
        ctx_copy(tile).wait()


def normalize(ctx_ref, inverse_ref, g_ref, o_ref):
    tokens, width = ctx_ref.shape
    gain = g_ref[...].astype(jnp.float32)
    for piece in range(tokens // LANES):
        rows = pl.ds(piece * LANES, LANES)
        turned = jnp.transpose(jnp.broadcast_to(inverse_ref[piece:piece + 1, :], (LANES, LANES)))
        for part in range(width // LANES):
            columns = pl.ds(part * LANES, LANES)
            o_ref[rows, columns] = (
                ctx_ref[rows, columns] * turned * gain[None, part * LANES:(part + 1) * LANES]
            ).astype(jnp.bfloat16)


def body(n_seq, n_head, query_rows, key_rows, value_rows, norm_gain):
    tokens, width = query_rows.shape
    heads = width // HEAD_DIM
    level_total = sum(tokens // 2**level for level in range(1, LEVELS + 1))
    coarse_all = tokens // TOP_POOL * n_seq
    keys = BLOCK + level_total + coarse_all
    vmem = pl.BlockSpec(memory_space=pltpu.VMEM)
    dma = pltpu.SemaphoreType.DMA
    context, inverse = pl.pallas_call(
        functools.partial(kernel, n_seq, n_head),
        out_shape=[
            jax.ShapeDtypeStruct((tokens, width), jnp.float32),
            jax.ShapeDtypeStruct((tokens // LANES, LANES), jnp.float32),
        ],
        in_specs=[pl.BlockSpec(memory_space=pl.ANY), vmem, vmem],
        out_specs=[pl.BlockSpec(memory_space=pl.ANY), vmem],
        scratch_shapes=[
            pltpu.VMEM((tokens, width), jnp.bfloat16),
            pltpu.VMEM((level_total, 2 * width), jnp.bfloat16),
            pltpu.VMEM((coarse_all + level_total, 2 * width), jnp.bfloat16),
            pltpu.VMEM((heads, tokens, 2 * LANES), jnp.float32),
            pltpu.VMEM((heads, tokens, LANES), jnp.float32),
            pltpu.VMEM((tokens, width), jnp.float32),
            pltpu.VMEM((n_head, tokens // LANES, LANES), jnp.float32),
            dma((LEVELS + 1,)),
            dma((LEVELS + 1,)),
            dma((n_seq,)),
            dma((n_seq,)),
            dma((n_head,)),
            dma((n_head,)),
            dma,
            dma((tokens // QUERY_TILE,)),
        ],
        compiler_params=pltpu.CompilerParams(
            collective_id=0, has_side_effects=True, vmem_limit_bytes=56 * 1024 * 1024
        ),
        cost_estimate=pl.CostEstimate(
            flops=4 * tokens * keys * width,
            bytes_accessed=8 * tokens * width,
            transcendentals=tokens * keys * heads,
        ),
    )(query_rows, key_rows, value_rows)
    return pl.pallas_call(
        normalize,
        out_shape=jax.ShapeDtypeStruct((tokens, width), jnp.bfloat16),
        in_specs=[vmem] * 3,
        out_specs=vmem,
        compiler_params=pltpu.CompilerParams(vmem_limit_bytes=16 * 1024 * 1024),
    )(context, inverse, norm_gain)


def solution(mesh):
    placed = (P("seq", "head"), P("seq", "head"), P("seq", "head"), P("head"))
    return jax.shard_map(
        functools.partial(body, mesh.shape["seq"], mesh.shape["head"]),
        mesh=mesh, in_specs=placed, out_specs=P("seq", "head"), check_vma=False,
    )
```
